256 devices in a mesh: row: 16 (over x, z_lo, core), col: 16 (over z_hi, y).
Axes of the slice: x: 4, y: 4, z: 8 (z_hi: 4, z_lo: 2; z = z_hi * 2 + z_lo), core: 2. Of those that a mesh axis runs over, the one named last changes fastest.
Arguments:
- points: float32 [131072, 32], P(('row', 'col')), may hold values from -6 to 6
- lengthscale: float32 [32], replicated, may hold values from 4 to 32
- weekday: int32 [131072], P(('row', 'col')), may hold values from 0 to 6
- solution: float32 [131072, 32], P(('row', 'col')), may hold values from -6 to 6
- residual: float32 [131072, 32], P(('row', 'col')), may hold values from -70 to 70
- direction: float32 [131072, 32], P(('row', 'col')), may hold values from -70 to 70
Outputs:
- new_solution: float32 [131072, 32], P(('row', 'col'))
- new_residual: float32 [131072, 32], P(('row', 'col'))
- new_direction: float32 [131072, 32], P(('row', 'col'))
The draws below stay inside these ranges and needn't reach their ends.
All inputs are finite; a program needn't handle non-finite values.
Results may differ from the reference program's by a relative error of at most 0.0068.
Values may be sent and summed in bfloat16 or wider, within the bound.
A program may use at most 64 MiB of HBM per device.

```python
import math
import jax
import jax.numpy as jnp
from jax import lax

FEAT = 32
PROBES = 32
DAYS = 7
PTS_DEV = 512
N = 131072


def state_scales(key):
    row_key, col_key = jax.random.split(key)
    position = jnp.arange(N, dtype=jnp.float32) / N
    trend = jnp.exp(math.log(3.0) * (position - 0.5))
    row_scale = trend * jnp.exp(jax.random.uniform(row_key, (N,), minval=-1.15, maxval=1.15))
    col_scale = jnp.exp(jax.random.uniform(col_key, (PROBES,), minval=-1.15, maxval=1.15))
    return row_scale[:, None] * col_scale[None, :]


def draw_residual(key, part):
    key = jax.random.fold_in(key, 11)
    scale_key, value_key = jax.random.split(key, 2)
    values = jnp.clip(jax.random.normal(value_key, (N, PROBES)), -4.0, 4.0)
    return (values * state_scales(scale_key)).astype(jnp.float32)


def draw_direction(key, part):
    key = jax.random.fold_in(key, 23)
    scale_key, value_key = jax.random.split(key, 2)
    values = jnp.clip(jax.random.normal(value_key, (N, PROBES)), -4.0, 4.0)
    return (values * state_scales(scale_key)).astype(jnp.float32)


def plant(drawn, own_key, least, top_value):
    longest = drawn.shape.index(max(drawn.shape))
    spots = []
    for shift in (0, 1):
        where = [jax.random.randint(jax.random.fold_in(own_key, axis), (), 0, length) for axis, length in enumerate(drawn.shape)]
        where[longest] = (where[longest] + shift) % drawn.shape[longest]
        spots.append(tuple(where))
    return drawn.at[spots[0]].set(least).at[spots[1]].set(top_value)


def levels(stream_key, extent, pieces, smallest, top_value):
    loudness, own = 1.0, jax.random.fold_in(stream_key, 6)
    for dim, parts in pieces:
        steps = jnp.exp(jax.random.uniform(jax.random.fold_in(own, dim), (parts,), jnp.float32, smallest / len(pieces), top_value / len(pieces)))
        loudness = loudness * jnp.repeat(steps, extent[dim] // parts).reshape([-1 if axis == dim else 1 for axis in range(len(extent))])
    return loudness


def normal_values(key, dims, deviation, bound, cuts=(), kind=jnp.bfloat16):
    loudness = levels(key, dims, cuts, -0.22, 0.18) if cuts else 1.0
    values = jax.random.normal(key, dims, jnp.float32) * deviation * loudness
    return jnp.minimum(jnp.maximum(values, -bound), bound).astype(kind)


def setup_inputs(seed: int = 0) -> dict:
    key_list = jax.random.split(jax.random.key(seed), 7)
    points = normal_values(key_list[0], (N, FEAT), 1.0, 6.0, ((0, 256),), jnp.float32)
    lengthscale = jnp.clip(jnp.exp(jax.random.uniform(key_list[1], (FEAT,), jnp.float32, math.log(4.0), math.log(32.0))), 4.0, 32.0)
    weekday = plant(jax.random.randint(key_list[2], (N,), 0, DAYS), jax.random.fold_in(key_list[2], 1), 0, DAYS - 1).astype(jnp.int32)
    solution = normal_values(key_list[3], (N, PROBES), 1.0, 6.0, ((0, 256),), jnp.float32)
    residual = draw_residual(jax.random.fold_in(key_list[6], 71), 0)
    direction = draw_direction(jax.random.fold_in(key_list[6], 71), 0)
    return {"points": points, "lengthscale": lengthscale, "weekday": weekday, "solution": solution, "residual": residual, "direction": direction}


root_five = 2.23606797749979
noise_level = 0.5
cross_day = 0.4

def kernel_block(left_scaled, left_norms, left_days, right_scaled, right_norms, right_days):
    inner_prod = jnp.dot(left_scaled, right_scaled.T, preferred_element_type=jnp.float32)
    squared = jnp.maximum(left_norms[:, None] + right_norms[None, :] - 2.0 * inner_prod, 0.0)
    scaled_dist = root_five * jnp.sqrt(squared)
    matern = (1.0 + scaled_dist + 5.0 / 3.0 * squared) * jnp.exp(-scaled_dist)
    factor = jnp.where(left_days[:, None] == right_days[None, :], 1.0, cross_day)
    return (matern * factor).astype(jnp.bfloat16)

def reference(points, lengthscale, weekday, solution, residual, direction):
    scaled = (points / lengthscale).astype(jnp.bfloat16)
    widened = scaled.astype(jnp.float32)
    norms = lax.optimization_barrier(jnp.sum(widened * widened, axis=1))
    half_direction = direction.astype(jnp.bfloat16)
    blocks = N // PTS_DEV
    block_scaled = scaled.reshape(blocks, PTS_DEV, FEAT)
    block_norms = norms.reshape(blocks, PTS_DEV)
    block_days = weekday.reshape(blocks, PTS_DEV)

    def one_block(block_args):
        left_scaled, left_norms, left_days = block_args
        kernel_tile = kernel_block(left_scaled, left_norms, left_days, scaled, norms, weekday)
        return jnp.dot(kernel_tile, half_direction, preferred_element_type=jnp.float32)
    applied = lax.map(one_block, (block_scaled, block_norms, block_days)).reshape(N, PROBES)
    image = applied + noise_level * direction
    old_norm = lax.optimization_barrier(jnp.sum(residual * residual, axis=0))
    curvature = lax.optimization_barrier(jnp.sum(direction * image, axis=0))
    step_length = old_norm / curvature
    new_solution = solution + step_length * direction
    new_residual = residual - step_length * image
    new_norm = lax.optimization_barrier(jnp.sum(new_residual * new_residual, axis=0))
    new_direction = new_residual + new_norm / old_norm * direction
    return (new_solution, new_residual, new_direction)
```

```python
import functools

import jax
import jax.numpy as jnp
from jax import lax
from jax.experimental import pallas as pl
from jax.experimental.pallas import tpu as pltpu
from jax.sharding import PartitionSpec as P

f32 = jnp.float32
bf16 = jnp.bfloat16
MESH = pl.DeviceIdType.MESH

root_five = 2.23606797749979
log2_e = 1.4426950408889634
noise_level = 0.5
cross_day = 0.4

MISC = 32
STEER = 48
PACK = 80
GROUP = 16
HALF = 8
OUT_SCALE = 5.0 / 3.0 * cross_day
SAME_DAY = 1.0 / cross_day


def kernel_values(squared, row_days, col_days):
    m = jnp.maximum(squared, 1e-30)
    u = m * lax.rsqrt(m)
    e = jnp.exp2(u * (-root_five * log2_e))
    p = (u + 3.0 / root_five) * u + 0.6
    k = (p * e).astype(bf16)
    return k * jnp.where(row_days == col_days, bf16(SAME_DAY), bf16(1.0))


def step_kernel(
    pts_ref, ls_ref, day_ref, sol_ref, res_ref, dir_ref,
    nsol_ref, nres_ref, ndir_ref,
    gcol, grow, xa, da, k0, k1, ro, co, srow, scol, rrow, rcol, stat, st1, st2,
    gc_send, gc_recv, gr_send, gr_recv, rr_send, rr_recv, rc_send, rc_recv,
    s1_send, s1_recv, s2_send, s2_recv,
):
    r = lax.axis_index("row")
    c = lax.axis_index("col")

    def at_row(d):
        return (lax.rem(r + d, GROUP), c)

    def at_col(d):
        return (r, lax.rem(c + d, GROUP))

    barrier = pltpu.get_barrier_semaphore()

    def greet(d, _):
        pl.semaphore_signal(barrier, inc=1, device_id=at_row(d), device_id_type=MESH)
        pl.semaphore_signal(barrier, inc=1, device_id=at_col(d), device_id_type=MESH)
        return 0

    lax.fori_loop(1, GROUP, greet, 0)

    def gather_col(d):
        return pltpu.make_async_remote_copy(
            src_ref=gcol.at[0], dst_ref=gcol.at[d], send_sem=gc_send.at[d],
            recv_sem=gc_recv.at[d], device_id=at_row(GROUP - d), device_id_type=MESH)

    def gather_row(d):
        return pltpu.make_async_remote_copy(
            src_ref=gcol.at[0], dst_ref=grow.at[d], send_sem=gr_send.at[d],
            recv_sem=gr_recv.at[d], device_id=at_col(GROUP - d), device_id_type=MESH)

    def give_row(d):
        return pltpu.make_async_remote_copy(
            src_ref=srow.at[d], dst_ref=rrow.at[d], send_sem=rr_send.at[d],
            recv_sem=rr_recv.at[d], device_id=at_col(d), device_id_type=MESH)

    def give_col(d):
        return pltpu.make_async_remote_copy(
            src_ref=scol.at[d], dst_ref=rcol.at[d], send_sem=rc_send.at[d],
            recv_sem=rc_recv.at[d], device_id=at_row(d), device_id_type=MESH)

    def share_row(d):
        return pltpu.make_async_remote_copy(
            src_ref=stat.at[0], dst_ref=st1.at[d], send_sem=s1_send.at[d],
            recv_sem=s1_recv.at[d], device_id=at_row(d), device_id_type=MESH)

    def share_col(d):
        return pltpu.make_async_remote_copy(
            src_ref=stat.at[1], dst_ref=st2.at[d], send_sem=s2_send.at[d],
            recv_sem=s2_recv.at[d], device_id=at_col(d), device_id_type=MESH)

    direction = dir_ref[...]
    scales = jnp.transpose(jnp.broadcast_to(ls_ref[...], (128, 32)))[:, :1]
    scaled = (pts_ref[...] / scales).astype(bf16)
    wide = scaled.astype(f32)
    norm = jnp.sum(wide * wide, axis=0, keepdims=True)
    norm_hi = norm.astype(bf16).astype(f32)
    rest = norm - norm_hi
    norm_mid = rest.astype(bf16).astype(f32)
    norm_lo = rest - norm_mid
    points = norm.shape[1]
    line = lax.broadcasted_iota(jnp.int32, (16, points), 0)
    misc = jnp.where(line == 0, norm_hi, 0.0)
    misc = jnp.where(line == 1, norm_mid, misc)
    misc = jnp.where(line == 2, norm_lo, misc)
    misc = jnp.where((line >= 3) & (line < 6), 1.0, misc)
    misc = jnp.where(line == 6, day_ref[...].astype(f32), misc)
    for own in (gcol, grow):
        own[0, :MISC, :] = scaled
        own[0, MISC:STEER, :] = misc.astype(bf16)
        own[0, STEER:, :] = direction.astype(bf16)

    ro[...] = jnp.zeros_like(ro)
    co[...] = jnp.zeros_like(co)

    def prepare(i):
        extra = grow[i, MISC:STEER, :].astype(f32)
        left = jnp.where(line < 3, 1.0, jnp.where(line < 6, pltpu.roll(extra, 3, 0), 0.0))
        block = jnp.concatenate(
            [grow[i, :MISC, :].astype(f32) * -2.0, left, jnp.zeros((128 - STEER, points), f32)], axis=0)
        xa[i] = jnp.transpose(block).astype(bf16)
        da[i] = jnp.transpose(jnp.broadcast_to(extra[6:7, :], (128, points))).astype(bf16)

    def fill(k, i, j):
        squared = jnp.dot(xa[i, :, :STEER], gcol[j, :STEER, :], preferred_element_type=f32)
        days = da[i]
        days = jnp.concatenate([days] * (points // 128), axis=1)
        k[...] = kernel_values(squared, days, gcol[j, MISC + 6:MISC + 7, :])

    def apply(k, i, j, kept):
        row_part = lax.dot_general(
            gcol[j, STEER:, :], k[...], (((1,), (1,)), ((), ())), preferred_element_type=f32)
        col_part = jnp.dot(grow[i, STEER:, :], k[...], preferred_element_type=f32)
        if kept is not None:
            row_part, col_part = row_part * kept, col_part * kept
        ro[i] += row_part
        co[j] += col_part

    def where_is(t):
        return t // GROUP, lax.rem(t, GROUP)

    prepare(0)
    pl.semaphore_wait(barrier, 2 * (GROUP - 1))

    def send_col(n, _):
        gather_col(n).start()
        return 0

    def send_row(n, _):
        gather_row(n).start()
        return 0

    lax.fori_loop(HALF, GROUP, send_col, 0)
    gather_row(1).start()
    lax.fori_loop(1, HALF, send_col, 0)
    lax.fori_loop(2, HALF + 1, send_row, 0)

    fill(k0, 0, 0)
    co[0] = jnp.dot(grow[0, STEER:, :], k0[...], preferred_element_type=f32)

    first, last = HALF, HALF * GROUP + HALF
    row_kept = jnp.where(r < HALF, 1.0, 0.0)
    col_kept = jnp.where(c < HALF, 1.0, 0.0)

    gather_col(HALF).wait_recv()
    fill(k0, 0, HALF)

    def arrive(t):
        i, j = where_is(t)

        @pl.when((t < GROUP) | ((t > GROUP) & (t < 2 * GROUP - HALF)))
        def _():
            gather_col(j).wait_recv()

    def leave(t):
        i, j = where_is(t)

        @pl.when((t > HALF * GROUP - HALF) & (t != HALF * GROUP))
        def _():
            scol[j] = co[j].astype(bf16)
            give_col(j).start()

    def two(m, _):
        t = first + 2 * m
        i0, j0 = where_is(t)
        i1, j1 = where_is(t + 1)
        i2, j2 = where_is(t + 2)
        arrive(t + 1)
        arrive(t + 2)

        @pl.when(j2 == 0)
        def _():
            gather_row(i2).wait_recv()
            prepare(i2)

        kept = jnp.where(t == first, row_kept, jnp.where(t == HALF * GROUP, col_kept, 1.0))
        fill(k1, i1, j1)
        apply(k0, i0, j0, kept)
        fill(k0, i2, j2)
        apply(k1, i1, j1, None)

        leave(t)
        leave(t + 1)

        @pl.when((j1 == GROUP - 1) & (i1 > 0))
        def _():
            srow[i1] = ro[i1].astype(bf16)
            give_row(i1).start()

        return 0

    lax.fori_loop(0, (last - first) // 2, two, 0)
    apply(k0, HALF, HALF, row_kept)
    scol[HALF] = co[HALF].astype(bf16)
    give_col(HALF).start()
    srow[HALF] = ro[HALF].astype(bf16)
    give_row(HALF).start()

    co[0] += ro[0]

    def take_row(d, _):
        give_row(d).wait_recv()
        co[0] += rrow[d].astype(f32)
        return 0

    def take_col(d, _):
        give_col(d).wait_recv()
        co[0] += rcol[d].astype(f32)
        return 0

    lax.fori_loop(1, HALF, take_row, 0)
    lax.fori_loop(HALF + 1, GROUP, take_col, 0)
    lax.fori_loop(1, HALF + 1, take_col, 0)
    take_row(HALF, 0)

    image = co[0] * OUT_SCALE + noise_level * direction
    residual = res_ref[...]
    lane = lax.broadcasted_iota(jnp.int32, (32, 128), 1)
    sums = [residual * residual, direction * image, residual * image, image * image]
    sums = [jnp.sum(v, axis=1, keepdims=True) for v in sums]
    packed = jnp.where(lane == 0, sums[0], jnp.where(lane == 1, sums[1], jnp.where(lane == 2, sums[2], sums[3])))

    def exchange(slot, packed, copy, landing):
        stat[slot] = packed

        def begin(d, _):
            copy(d).start()
            return 0

        def take(d, total):
            copy(d).wait_recv()
            return total + landing[d]

        lax.fori_loop(1, GROUP, begin, 0)
        return lax.fori_loop(1, GROUP, take, packed)

    packed = exchange(0, packed, share_row, st1)
    packed = exchange(1, packed, share_col, st2)
    old_norm, curvature, mixed, image_norm = (packed[:, n:n + 1] for n in range(4))
    step = old_norm / curvature
    new_norm = old_norm - 2.0 * step * mixed + step * step * image_norm
    new_residual = residual - step * image
    nsol_ref[...] = sol_ref[...] + step * direction
    nres_ref[...] = new_residual
    ndir_ref[...] = new_residual + new_norm / old_norm * direction

    def finish(d, _):
        gather_col(d).wait_send()
        give_col(d).wait_send()
        share_row(d).wait_send()
        share_col(d).wait_send()
        return 0

    def finish_row(d, _):
        gather_row(d).wait_send()
        give_row(d).wait_send()
        return 0

    lax.fori_loop(1, GROUP, finish, 0)
    lax.fori_loop(1, HALF + 1, finish_row, 0)


def per_device(points, lengthscale, weekday, solution, residual, direction):
    count, feats = points.shape
    probes = direction.shape[1]
    out = jax.ShapeDtypeStruct((probes, count), f32)
    dma = pltpu.SemaphoreType.DMA
    vmem = pltpu.VMEM
    outs = pl.pallas_call(
        step_kernel,
        out_shape=[out] * 3,
        in_specs=[pl.BlockSpec(memory_space=vmem)] * 6,
        out_specs=[pl.BlockSpec(memory_space=vmem)] * 3,
        scratch_shapes=[
            vmem((GROUP, PACK, count), bf16),
            vmem((HALF + 1, PACK, count), bf16),
            vmem((HALF + 1, count, 128), bf16),
            vmem((HALF + 1, count, 128), bf16),
            vmem((count, count), bf16),
            vmem((count, count), bf16),
            vmem((HALF + 1, probes, count), f32),
            vmem((GROUP, probes, count), f32),
            vmem((HALF + 1, probes, count), bf16),
            vmem((GROUP, probes, count), bf16),
            vmem((HALF + 1, probes, count), bf16),
            vmem((GROUP, probes, count), bf16),
            vmem((2, probes, 128), f32),
            vmem((GROUP, probes, 128), f32),
            vmem((GROUP, probes, 128), f32),
            dma((GROUP,)), dma((GROUP,)), dma((HALF + 1,)), dma((HALF + 1,)),
            dma((HALF + 1,)), dma((HALF + 1,)), dma((GROUP,)), dma((GROUP,)),
            dma((GROUP,)), dma((GROUP,)), dma((GROUP,)), dma((GROUP,)),
        ],
        compiler_params=pltpu.CompilerParams(
            collective_id=0, has_side_effects=True, vmem_limit_bytes=48 * 2**20),
        name="cg_step",
    )(points.T, lengthscale[None, :], weekday[None, :], solution.T, residual.T, direction.T)
    return tuple(v.T for v in outs)


def solution(mesh):
    split = P(("row", "col"), None)
    in_specs = (split, P(), P(("row", "col")), split, split, split)
    return jax.shard_map(
        per_device, mesh=mesh, in_specs=in_specs, out_specs=(split, split, split), check_vma=False
    )
```

```python
import functools

import jax
import jax.numpy as jnp
from jax import lax
from jax.experimental import pallas as pl
from jax.experimental.pallas import tpu as pltpu
from jax.sharding import PartitionSpec as P

f32 = jnp.float32
bf16 = jnp.bfloat16
MESH = pl.DeviceIdType.MESH

root_five = 2.23606797749979
log2_e = 1.4426950408889634
noise_level = 0.5
cross_day = 0.4

FEATS = 32
MISC = 64
SENT = 80
PACK = 112
DEPTH = PACK - FEATS
GROUP = 16
HALF = 8
STRETCH = 5.0 / 3.0 * log2_e
X_PER_ROOT = -(3.0 * log2_e) ** 0.5
OUT_SCALE = cross_day / log2_e
SAME_DAY = 1.0 / cross_day
LONG = 81
TILES = 129
TINY = 1e-30


def kernel_values(m, row_days, col_days):
    x = (m * lax.rsqrt(m)) * X_PER_ROOT
    e = jnp.exp2(x)
    k = (((m + log2_e) - x) * e).astype(bf16)
    return k * jnp.where(row_days == col_days, bf16(SAME_DAY), bf16(1.0))


def step_kernel(
    pts_any, ls_any, day_any, sol_any, res_any, dir_any,
    nsol_ref, nres_ref, ndir_ref,
    pts_ref, ls_ref, day_ref, sol_ref, res_ref, dir_ref, load,
    gcol, grow, xa, da, v0, v1, k0, k1, ro, co, rrow, rcol, stat, st1, st2,
    gc_send, gc_recv, fw_send, gr_send, gr_recv, rr_send, rr_recv, rc_send, rc_recv,
    s1_send, s1_recv, s2_send, s2_recv,
):
    r = lax.axis_index("row")
    c = lax.axis_index("col")

    def at_row(d):
        return (lax.rem(r + d, GROUP), c)

    def at_col(d):
        return (r, lax.rem(c + d + GROUP, GROUP))

    loads = [
        pltpu.make_async_copy(src, dst, load.at[n])
        for n, (src, dst) in enumerate((
            (ls_any, ls_ref), (pts_any, pts_ref), (day_any, day_ref),
            (dir_any, dir_ref), (res_any, res_ref), (sol_any, sol_ref)))
    ]
    for copy in loads:
        copy.start()

    barrier = pltpu.get_barrier_semaphore()

    def greet(d, _):
        pl.semaphore_signal(barrier, inc=1, device_id=at_row(d), device_id_type=MESH)
        pl.semaphore_signal(barrier, inc=1, device_id=at_col(d), device_id_type=MESH)
        return 0

    lax.fori_loop(1, GROUP, greet, 0)

    sent = pl.ds(0, SENT)

    def gather_col(d):
        return pltpu.make_async_remote_copy(
            src_ref=gcol.at[0, sent], dst_ref=gcol.at[d, sent], send_sem=gc_send,
            recv_sem=gc_recv.at[d], device_id=at_row(GROUP - d), device_id_type=MESH)

    side = 1 - 2 * lax.rem(r, 2)

    def forward(d):
        slot = lax.rem(d - side + GROUP, GROUP)
        return pltpu.make_async_remote_copy(
            src_ref=gcol.at[d, sent], dst_ref=gcol.at[slot, sent], send_sem=fw_send,
            recv_sem=gc_recv.at[slot], device_id=at_row(side + GROUP), device_id_type=MESH)

    def turn(d):
        return d * (2 * lax.rem(d, 2) - 1)

    def gather_row(d):
        return pltpu.make_async_remote_copy(
            src_ref=gcol.at[0, sent], dst_ref=grow.at[d], send_sem=gr_send,
            recv_sem=gr_recv.at[d], device_id=at_col(-turn(d)), device_id_type=MESH)

    def give_row(d):
        return pltpu.make_async_remote_copy(
            src_ref=ro.at[d], dst_ref=rrow.at[d], send_sem=rr_send,
            recv_sem=rr_recv, device_id=at_col(turn(d)), device_id_type=MESH)

    def give_col(d):
        return pltpu.make_async_remote_copy(
            src_ref=co.at[d], dst_ref=rcol.at[d], send_sem=rc_send,
            recv_sem=rc_recv, device_id=at_row(d), device_id_type=MESH)

    def share_row(d):
        return pltpu.make_async_remote_copy(
            src_ref=stat.at[0], dst_ref=st1.at[d], send_sem=s1_send,
            recv_sem=s1_recv, device_id=at_row(d), device_id_type=MESH)

    def share_col(d):
        return pltpu.make_async_remote_copy(
            src_ref=stat.at[1], dst_ref=st2.at[d], send_sem=s2_send,
            recv_sem=s2_recv, device_id=at_col(d), device_id_type=MESH)

    for copy in loads[:4]:
        copy.wait()
    direction = dir_ref[...]
    scales = jnp.transpose(jnp.broadcast_to(ls_ref[...], (128, 32)))[:, :1]
    scaled = (pts_ref[...] / scales).astype(bf16)
    wide = scaled.astype(f32)
    norm = jnp.sum(wide * wide, axis=0, keepdims=True) * STRETCH
    norm_hi = norm.astype(bf16).astype(f32)
    rest = norm - norm_hi
    norm_mid = rest.astype(bf16).astype(f32)
    norm_lo = rest - norm_mid
    points = norm.shape[1]
    line = lax.broadcasted_iota(jnp.int32, (16, points), 0)
    misc = jnp.where(line == 0, norm_hi, 0.0)
    misc = jnp.where(line == 1, norm_mid, misc)
    misc = jnp.where(line == 2, norm_lo, misc)
    misc = jnp.where((line >= 3) & (line < 6), 1.0, misc)
    misc = jnp.where(line == 6, day_ref[...].astype(f32), misc)
    for own in (gcol, grow):
        own[0, :FEATS, :] = direction.astype(bf16)
        own[0, FEATS:MISC, :] = scaled
        own[0, MISC:SENT, :] = misc.astype(bf16)
    gcol[0, SENT:, :] = scaled

    ro[...] = jnp.zeros_like(ro)
    co[...] = jnp.zeros_like(co)

    def prepare(i):
        extra = grow[i, MISC:SENT, :].astype(f32)
        ones = jnp.where(line < 3, 1.0, jnp.where(line < 6, pltpu.roll(extra, 3, 0), 0.0))
        left = grow[i, FEATS:MISC, :].astype(f32) * (-2.0 * STRETCH)
        high = left.astype(bf16).astype(f32)
        block = jnp.concatenate(
            [high, ones, left - high, jnp.zeros((128 - DEPTH, points), f32)], axis=0)
        xa[i] = jnp.transpose(block).astype(bf16)
        da[i] = jnp.transpose(jnp.broadcast_to(extra[6:7, :], (128, points))).astype(bf16)

    rows = points // 2
    halves = (slice(0, rows), slice(rows, points))

    def distances(v, i, j, h):
        squared = jnp.dot(xa[i, halves[h], :DEPTH], gcol[j, FEATS:, :], preferred_element_type=f32)
        v[...] = jnp.maximum(squared, TINY)

    def values(v, k, i, j, h):
        days = jnp.concatenate([da[i, halves[h], :]] * (points // 128), axis=1)
        k[...] = kernel_values(v[...], days, gcol[j, MISC + 6:MISC + 7, :])

    def apply(k, i, j, h, kept=None):
        row_part = lax.dot_general(
            gcol[j, :FEATS, :], k[...], (((1,), (1,)), ((), ())), preferred_element_type=f32)
        col_part = jnp.dot(grow[i, :FEATS, halves[h]], k[...], preferred_element_type=f32)
        if kept is not None:
            row_part, col_part = row_part * kept, col_part * kept
        ro[i, :, halves[h]] += row_part
        co[j] += col_part

    def where_is(t):
        p = lax.rem(t + HALF, GROUP)
        q = lax.rem(p, HALF)
        line = lax.div(t + HALF, GROUP)
        turned = t - LONG
        return (
            jnp.where(t < HALF, 0, jnp.where(t < LONG, 3 + line, 1 + lax.div(lax.rem(turned, 12), 4))),
            jnp.where(t < LONG, p - q + lax.rem(2 * q, HALF) + lax.div(q, 4),
                      lax.rem(4 * lax.div(turned, 12) + lax.rem(turned, 4) + 1, GROUP)))

    prepare(0)
    for h in range(2):
        distances(v0, 0, 0, h)
        values(v0, k0, 0, 0, h)
        co[0] += jnp.dot(grow[0, :FEATS, halves[h]], k0[...], preferred_element_type=f32)
    k1[...] = jnp.zeros_like(k1)

    pl.semaphore_wait(barrier, 2 * (GROUP - 1))

    def send_col(n, _):
        gather_col(2 * n).start()
        return 0

    forward(0).start()
    lax.fori_loop(HALF // 2, HALF, send_col, 0)
    gather_row(4).start()
    lax.fori_loop(1, HALF // 2, send_col, 0)

    row_kept = jnp.where(r < HALF, 1.0, 0.0)
    col_kept = jnp.where(c < HALF, 1.0, 0.0)

    def arrived(j):
        gather_col(j).wait_recv()
        gcol[j, SENT:, :] = gcol[j, FEATS:MISC, :]

        @pl.when(lax.rem(j, 2) == 0)
        def _():
            forward(j).start()

    arrived(HALF)
    distances(v0, 0, HALF, 0)

    def two(m, places):
        t = 2 * m
        i_, j_, i0, j0 = places
        i1, j1 = where_is(t + 1)
        i2, j2 = where_is(t + 2)

        @pl.when(t < LONG)
        def _():
            @pl.when(t < GROUP)
            def _():
                arrived(j1)

                @pl.when((t != HALF - 2) & (t != GROUP - 2))
                def _():
                    arrived(j2)

            @pl.when(lax.rem(t, GROUP) == HALF - 2)
            def _():
                gather_row(i2).wait_recv()

                @pl.when(i2 < HALF)
                def _():
                    gather_row(i2 + 1).start()

                @pl.when(i2 == HALF - 1)
                def _():
                    for n in (1, 2, 3):
                        gather_row(n).start()

                @pl.when(i2 > 5)
                def _():
                    give_row(i2 - 2).start()

                prepare(i2)

            @pl.when(t == LONG - 1)
            def _():
                def ready(n, _):
                    gather_row(n).wait_recv()
                    prepare(n)
                    return 0

                lax.fori_loop(1, 4, ready, 0)
                give_row(7).start()

        kept = jnp.where((t == 0) | (t == LONG - 1), row_kept, jnp.where(t == LONG - 9, col_kept, 1.0))
        apply(k1, i_, j_, 1)
        distances(v1, i0, j0, 1)
        values(v0, k0, i0, j0, 0)
        apply(k0, i0, j0, 0, kept)
        distances(v0, i1, j1, 0)
        values(v1, k1, i0, j0, 1)
        apply(k1, i0, j0, 1, kept)
        distances(v1, i1, j1, 1)
        values(v0, k0, i1, j1, 0)
        apply(k0, i1, j1, 0)
        distances(v0, i2, j2, 0)
        values(v1, k1, i1, j1, 1)

        @pl.when(t >= LONG - 1)
        def _():
            @pl.when((i_ == 3) & (j_ != 0))
            def _():
                give_col(j_).start()

            @pl.when((i0 == 3) & (j0 != 0))
            def _():
                give_col(j0).start()

            for n, done in ((8, LONG - 1), (1, TILES - 9), (2, TILES - 5)):
                @pl.when(t == done)
                def _(n=n):
                    give_row(n).start()

        return i1, j1, i2, j2

    begin = jnp.int32(0)
    lax.fori_loop(0, TILES // 2, two, (begin, begin, begin, begin + HALF))
    apply(k1, 3, GROUP - 1, 1)
    distances(v1, 3, 0, 1)
    values(v0, k0, 3, 0, 0)
    give_col(GROUP - 1).start()
    apply(k0, 3, 0, 0)
    values(v1, k1, 3, 0, 1)
    apply(k1, 3, 0, 1)
    give_row(3).start()

    def all_of(ref, count, sem):
        part = ref.at[pl.ds(1, count)]
        pltpu.make_async_copy(part, part, sem).wait()

    all_of(rcol, GROUP - 1, rc_recv)
    all_of(rrow, HALF, rr_recv)
    applied = ro[0] + co[0]
    for n in range(1, GROUP):
        applied = applied + rcol[n]
    for n in range(1, HALF + 1):
        applied = applied + rrow[n]

    image = applied * OUT_SCALE + noise_level * direction
    for copy in loads[4:]:
        copy.wait()
    residual = res_ref[...]
    lane = lax.broadcasted_iota(jnp.int32, (32, 128), 1)
    blank = jnp.zeros((96, 128), f32)
    sums = [residual * residual, direction * image, residual * image, image * image]
    sums = [jnp.sum(v, axis=1, keepdims=True) for v in sums]
    packed = jnp.where(lane == 0, sums[0], jnp.where(lane == 1, sums[1], jnp.where(lane == 2, sums[2], sums[3])))

    def exchange(slot, packed, copy, landing, sem):
        stat[slot] = packed

        def begin(d, _):
            copy(d).start()
            return 0

        lax.fori_loop(1, GROUP, begin, 0)
        all_of(landing, GROUP - 1, sem)
        for n in range(1, GROUP):
            packed = packed + landing[n]
        return packed

    packed = jnp.transpose(jnp.concatenate([packed, blank], axis=0))[:8]
    packed = exchange(0, packed, share_row, st1, s1_recv)
    packed = exchange(1, packed, share_col, st2, s2_recv)
    packed = jnp.transpose(jnp.concatenate([packed, blank, blank[:24]], axis=0))[:32]
    old_norm, curvature, mixed, image_norm = (packed[:, n:n + 1] for n in range(4))
    step = old_norm / curvature
    new_norm = old_norm - 2.0 * step * mixed + step * step * image_norm
    new_residual = residual - step * image
    nsol_ref[...] = sol_ref[...] + step * direction
    nres_ref[...] = new_residual
    ndir_ref[...] = new_residual + new_norm / old_norm * direction

    def all_sent(ref, count, sem):
        part = ref.at[pl.ds(0, count)]
        pltpu.make_async_copy(part, part, sem).wait()

    all_sent(grow, HALF - 1, gc_send)
    all_sent(grow, HALF, gr_send)
    all_sent(grow, HALF, fw_send)
    all_sent(co, GROUP - 1, rc_send)
    all_sent(ro, HALF, rr_send)
    all_sent(st1, GROUP - 1, s1_send)
    all_sent(st2, GROUP - 1, s2_send)


def per_device(points, lengthscale, weekday, solution, residual, direction):
    count, feats = points.shape
    probes = direction.shape[1]
    out = jax.ShapeDtypeStruct((probes, count), f32)
    dma = pltpu.SemaphoreType.DMA
    vmem = pltpu.VMEM
    outs = pl.pallas_call(
        step_kernel,
        out_shape=[out] * 3,
        in_specs=[pl.BlockSpec(memory_space=pl.ANY)] * 6,
        out_specs=[pl.BlockSpec(memory_space=vmem)] * 3,
        scratch_shapes=[
            vmem((feats, count), f32), vmem((1, feats), f32), vmem((1, count), jnp.int32),
            vmem((probes, count), f32), vmem((probes, count), f32), vmem((probes, count), f32),
            dma((6,)),
            vmem((GROUP, PACK, count), bf16),
            vmem((HALF + 1, SENT, count), bf16),
            vmem((HALF + 1, count, 128), bf16),
            vmem((HALF + 1, count, 128), bf16),
            vmem((count // 2, count), f32),
            vmem((count // 2, count), f32),
            vmem((count // 2, count), bf16),
            vmem((count // 2, count), bf16),
            vmem((HALF + 1, probes, count), f32),
            vmem((GROUP, probes, count), f32),
            vmem((HALF + 1, probes, count), f32),
            vmem((GROUP, probes, count), f32),
            vmem((2, 8, 128), f32),
            vmem((GROUP, 8, 128), f32),
            vmem((GROUP, 8, 128), f32),
            dma, dma((GROUP,)), dma, dma, dma((HALF + 1,)),
            dma, dma, dma, dma, dma, dma, dma, dma,
        ],
        compiler_params=pltpu.CompilerParams(
            collective_id=0, has_side_effects=True, vmem_limit_bytes=48 * 2**20),
        name="cg_step",
    )(points.T, lengthscale[None, :], weekday[None, :], solution.T, residual.T, direction.T)
    return tuple(v.T for v in outs)


def solution(mesh):
    split = P(("row", "col"), None)
    in_specs = (split, P(), P(("row", "col")), split, split, split)
    return jax.shard_map(
        per_device, mesh=mesh, in_specs=in_specs, out_specs=(split, split, split), check_vma=False
    )
```

```python
import functools

import jax
import jax.numpy as jnp
from jax import lax
from jax.experimental import pallas as pl
from jax.experimental.pallas import tpu as pltpu
from jax.sharding import PartitionSpec as P

f32 = jnp.float32
bf16 = jnp.bfloat16
MESH = pl.DeviceIdType.MESH

root_five = 2.23606797749979
log2_e = 1.4426950408889634
noise_level = 0.5
cross_day = 0.4

FEATS = 32
MISC = 64
SENT = 80
PACK = 112
DEPTH = PACK - FEATS
GROUP = 16
HALF = 8
STRETCH = 5.0 / 3.0 * log2_e
X_PER_ROOT = -(3.0 * log2_e) ** 0.5
OUT_SCALE = cross_day / log2_e
SAME_DAY = 1.0 / cross_day
AWAY = HALF + 1
FAR = 1e6
LONG = 81
TILES = 129
LATE = 13
TINY = 1e-30


def kernel_values(m, row_days, col_days):
    x = (m * lax.rsqrt(m)) * X_PER_ROOT
    e = jnp.exp2(x)
    k = (((m + log2_e) - x) * e).astype(bf16)
    return k * jnp.where(row_days == col_days, bf16(SAME_DAY), bf16(1.0))


def step_kernel(
    pts_any, ls_any, day_any, res_any, dir_any,
    image_ref, factors_ref,
    pts_ref, ls_ref, day_ref, res_ref, dir_ref, load,
    gcol, grow, xa, da, v0, v1, k0, k1, ro, co, rrow, rcol, late, landed, stat, st1, st2,
    gc_send, gc_recv, fw_send, gr_send, gr_recv, rr_send, rr_recv, rc_send, rc_recv,
    s1_send, s1_recv, s2_send, s2_recv, late_send, late_recv,
):
    r = lax.axis_index("row")
    c = lax.axis_index("col")

    def at_row(d):
        return (lax.rem(r + d, GROUP), c)

    def at_col(d):
        return (r, lax.rem(c + d + GROUP, GROUP))

    loads = [
        pltpu.make_async_copy(src, dst, load.at[n])
        for n, (src, dst) in enumerate((
            (ls_any, ls_ref), (pts_any, pts_ref), (day_any, day_ref),
            (dir_any, dir_ref), (res_any, res_ref)))
    ]
    for copy in loads:
        copy.start()

    barrier = pltpu.get_barrier_semaphore()

    def greet(d, _):
        pl.semaphore_signal(barrier, inc=1, device_id=at_row(d), device_id_type=MESH)
        pl.semaphore_signal(barrier, inc=1, device_id=at_col(d), device_id_type=MESH)
        return 0

    lax.fori_loop(1, GROUP, greet, 0)

    sent = pl.ds(0, SENT)

    def gather_col(d):
        return pltpu.make_async_remote_copy(
            src_ref=gcol.at[0, sent], dst_ref=gcol.at[d, sent], send_sem=gc_send,
            recv_sem=gc_recv.at[d], device_id=at_row(GROUP - d), device_id_type=MESH)

    side = 1 - 2 * lax.rem(r, 2)

    def forward(d):
        slot = lax.rem(d - side + GROUP, GROUP)
        return pltpu.make_async_remote_copy(
            src_ref=gcol.at[d, sent], dst_ref=gcol.at[slot, sent], send_sem=fw_send,
            recv_sem=gc_recv.at[slot], device_id=at_row(side + GROUP), device_id_type=MESH)

    def turn(d):
        return d * (2 * lax.rem(d, 2) - 1)

    def gather_row(d):
        return pltpu.make_async_remote_copy(
            src_ref=gcol.at[0, sent], dst_ref=grow.at[d], send_sem=gr_send,
            recv_sem=gr_recv.at[d], device_id=at_col(-turn(d)), device_id_type=MESH)

    def give_row(d):
        return pltpu.make_async_remote_copy(
            src_ref=ro.at[d], dst_ref=rrow.at[d], send_sem=rr_send,
            recv_sem=rr_recv, device_id=at_col(turn(d)), device_id_type=MESH)

    def give_col(d):
        return pltpu.make_async_remote_copy(
            src_ref=co.at[d], dst_ref=rcol.at[d], send_sem=rc_send,
            recv_sem=rc_recv, device_id=at_row(d), device_id_type=MESH)

    def give_late(n, ref, d, place):
        late[n] = ref[d].astype(bf16)
        pltpu.make_async_remote_copy(
            src_ref=late.at[n], dst_ref=landed.at[n], send_sem=late_send,
            recv_sem=late_recv, device_id=place, device_id_type=MESH).start()

    def late_row(d):
        give_late(d - 1, ro, d, at_col(turn(d)))

    def late_col(d):
        give_late(d - LATE + 3, co, d, at_row(d))

    def share_row(d):
        return pltpu.make_async_remote_copy(
            src_ref=stat.at[0], dst_ref=st1.at[d], send_sem=s1_send,
            recv_sem=s1_recv, device_id=at_row(d), device_id_type=MESH)

    def share_col(d):
        return pltpu.make_async_remote_copy(
            src_ref=stat.at[1], dst_ref=st2.at[d], send_sem=s2_send,
            recv_sem=s2_recv, device_id=at_col(d), device_id_type=MESH)

    for copy in loads[:4]:
        copy.wait()
    direction = dir_ref[...]
    scales = jnp.transpose(jnp.broadcast_to(ls_ref[...], (128, 32)))[:, :1]
    scaled = (pts_ref[...] / scales).astype(bf16)
    wide = scaled.astype(f32)
    norm = jnp.sum(wide * wide, axis=0, keepdims=True) * STRETCH
    norm_hi = norm.astype(bf16).astype(f32)
    rest = norm - norm_hi
    norm_mid = rest.astype(bf16).astype(f32)
    norm_lo = rest - norm_mid
    points = norm.shape[1]
    line = lax.broadcasted_iota(jnp.int32, (16, points), 0)
    misc = jnp.where(line == 0, norm_hi, 0.0)
    misc = jnp.where(line == 1, norm_mid, misc)
    misc = jnp.where(line == 2, norm_lo, misc)
    misc = jnp.where((line >= 3) & (line < 6), 1.0, misc)
    misc = jnp.where(line == 6, day_ref[...].astype(f32), misc)
    for own in (gcol, grow):
        own[0, :FEATS, :] = direction.astype(bf16)
        own[0, FEATS:MISC, :] = scaled
        own[0, MISC:SENT, :] = misc.astype(bf16)
    gcol[0, SENT:, :] = scaled

    ro[...] = jnp.zeros_like(ro)
    co[...] = jnp.zeros_like(co)

    def prepare(i):
        extra = grow[i, MISC:SENT, :].astype(f32)
        ones = jnp.where(line < 3, 1.0, jnp.where(line < 6, pltpu.roll(extra, 3, 0), 0.0))
        left = grow[i, FEATS:MISC, :].astype(f32) * (-2.0 * STRETCH)
        high = left.astype(bf16).astype(f32)
        block = jnp.concatenate(
            [high, ones, left - high, jnp.zeros((128 - DEPTH, points), f32)], axis=0)
        xa[i] = jnp.transpose(block).astype(bf16)
        da[i] = jnp.transpose(jnp.broadcast_to(extra[6:7, :], (128, points))).astype(bf16)

    rows = points // 2
    halves = (slice(0, rows), slice(rows, points))

    def distances(v, i, j, h):
        squared = jnp.dot(xa[i, halves[h], :DEPTH], gcol[j, FEATS:, :], preferred_element_type=f32)
        v[...] = jnp.maximum(squared, TINY)

    def values(v, k, i, j, h):
        days = jnp.concatenate([da[i, halves[h], :]] * (points // 128), axis=1)
        k[...] = kernel_values(v[...], days, gcol[j, MISC + 6:MISC + 7, :])

    def apply(k, i, j, h):
        row_part = lax.dot_general(
            gcol[j, :FEATS, :], k[...], (((1,), (1,)), ((), ())), preferred_element_type=f32)
        col_part = jnp.dot(grow[i, :FEATS, halves[h]], k[...], preferred_element_type=f32)
        ro[i, :, halves[h]] += row_part
        co[j] += col_part

    def early_place(t):
        p = lax.rem(t + HALF, GROUP)
        q = lax.rem(p, HALF)
        line = lax.div(t + HALF, GROUP)
        shift = jnp.where(t < HALF, 4, 0)
        return (
            jnp.where(t < HALF, 0, 3 + line),
            p - q + lax.rem(2 * q + shift, HALF) + lax.div(q, 4))

    def late_place(t):
        turned = lax.rem(t - LONG, 12)
        return (
            1 + lax.div(turned, 4),
            lax.rem(4 * lax.div(t - LONG, 12) + lax.rem(turned, 4) + 1, GROUP))

    prepare(0)
    for h in range(2):
        distances(v0, 0, 0, h)
        values(v0, k0, 0, 0, h)
        co[0] += jnp.dot(grow[0, :FEATS, halves[h]], k0[...], preferred_element_type=f32)
    k1[...] = jnp.zeros_like(k1)
    lane = lax.broadcasted_iota(jnp.int32, (points, 128), 1)
    xa[AWAY] = jnp.where(lane == MISC - FEATS + 3, FAR, 0.0).astype(bf16)

    pl.semaphore_wait(barrier, 2 * (GROUP - 1))

    def send_col(n, _):
        gather_col(2 * n).start()
        return 0

    forward(0).start()
    for n in (6, 7, 4, 5):
        send_col(n, 0)
    gather_row(4).start()
    lax.fori_loop(1, HALF // 2, send_col, 0)

    def left_of(t, i):
        along_row = (t == 2) | (t == LONG - 1)
        gone = (along_row & (r >= HALF)) | ((t == LONG - 9) & (c >= HALF))
        return jnp.where(gone, AWAY, i)

    def arrived(j):
        gather_col(j).wait_recv()
        gcol[j, SENT:, :] = gcol[j, FEATS:MISC, :]

        @pl.when(lax.rem(j, 2) == 0)
        def _():
            forward(j).start()

    arrived(HALF + 4)
    distances(v0, 0, HALF + 4, 0)

    def early(m, places):
        t = 2 * m
        tile1 = i1, j1 = early_place(t + 1)
        i2, j2 = early_place(t + 2)

        @pl.when(t < GROUP)
        def _():
            arrived(j1)

            @pl.when((t != HALF - 2) & (t != GROUP - 2))
            def _():
                arrived(j2)

        @pl.when(lax.rem(t, GROUP) == HALF - 2)
        def _():
            gather_row(i2).wait_recv()

            @pl.when(i2 < HALF)
            def _():
                gather_row(i2 + 1).start()

            @pl.when(i2 == HALF - 1)
            def _():
                for n in (1, 2, 3):
                    gather_row(n).start()

            @pl.when(i2 > 5)
            def _():
                give_row(i2 - 2).start()

            prepare(i2)

        left2 = left_of(t + 2, i2)
        two_tiles(places, tile1, (left2, i2, j2))
        return i1, j1, left2, i2, j2

    def two_tiles(places, tile1, tile2):
        i_, j_, left0, i0, j0 = places
        i1, j1 = tile1
        left2, i2, j2 = tile2

        apply(k1, i_, j_, 1)
        distances(v1, left0, j0, 1)
        values(v0, k0, i0, j0, 0)
        apply(k0, i0, j0, 0)
        distances(v0, i1, j1, 0)
        values(v1, k1, i0, j0, 1)
        apply(k1, i0, j0, 1)
        distances(v1, i1, j1, 1)
        values(v0, k0, i1, j1, 0)
        apply(k0, i1, j1, 0)
        distances(v0, left2, j2, 0)
        values(v1, k1, i1, j1, 1)

    def late_tiles(m, places):
        t = 2 * m
        i_, j_, _, i0, j0 = places
        tile1 = i1, j1 = late_place(t + 1)
        i2, j2 = late_place(t + 2)
        two_tiles(places, tile1, (i2, i2, j2))

        for i, j in ((i_, j_), (i0, j0)):
            @pl.when((i == 3) & (j < LATE))
            def _(j=j):
                give_col(j).start()

        for done, send in (
            (LONG - 1, lambda: give_row(8).start()),
            (TILES - 9, lambda: late_row(1)),
            (TILES - 5, lambda: late_row(2)),
            (TILES - 3, lambda: (late_col(LATE), late_col(LATE + 1))),
        ):
            pl.when(t == done)(lambda send=send: (send(), None)[1])

        return i1, j1, i2, i2, j2

    begin = jnp.int32(0)
    places = (begin, begin, begin, begin, begin + HALF + 4)
    places = lax.fori_loop(0, LONG // 2, early, places)
    for n in (1, 2, 3):
        gather_row(n).wait_recv()
        prepare(n)
    give_row(7).start()
    lax.fori_loop(LONG // 2, TILES // 2, late_tiles, places)
    apply(k1, 3, GROUP - 1, 1)
    distances(v1, 3, 0, 1)
    values(v0, k0, 3, 0, 0)
    late_col(GROUP - 1)
    apply(k0, 3, 0, 0)
    values(v1, k1, 3, 0, 1)
    apply(k1, 3, 0, 1)
    late_row(3)

    def all_of(ref, start, count, sem):
        part = ref.at[pl.ds(start, count)]
        pltpu.make_async_copy(part, part, sem).wait()

    all_of(rcol, 1, LATE - 1, rc_recv)
    all_of(rrow, 4, HALF - 3, rr_recv)
    applied = ro[0] + co[0]
    for n in range(1, LATE):
        applied = applied + rcol[n]
    for n in range(4, HALF + 1):
        applied = applied + rrow[n]
    all_of(landed, 0, 6, late_recv)
    for n in range(6):
        applied = applied + landed[n].astype(f32)

    image = applied * OUT_SCALE + noise_level * direction
    for copy in loads[4:]:
        copy.wait()
    residual = res_ref[...]
    lane = lax.broadcasted_iota(jnp.int32, (32, 128), 1)
    blank = jnp.zeros((96, 128), f32)
    sums = [residual * residual, direction * image, residual * image, image * image]
    sums = [jnp.sum(v, axis=1, keepdims=True) for v in sums]
    packed = jnp.where(lane == 0, sums[0], jnp.where(lane == 1, sums[1], jnp.where(lane == 2, sums[2], sums[3])))

    def exchange(slot, packed, copy, landing, sem):
        stat[slot] = packed

        def begin(d, _):
            copy(d).start()
            return 0

        lax.fori_loop(1, GROUP, begin, 0)
        all_of(landing, 1, GROUP - 1, sem)
        for n in range(1, GROUP):
            packed = packed + landing[n]
        return packed

    packed = jnp.transpose(jnp.concatenate([packed, blank], axis=0))[:8]
    packed = exchange(0, packed, share_row, st1, s1_recv)
    packed = exchange(1, packed, share_col, st2, s2_recv)
    packed = jnp.transpose(jnp.concatenate([packed, blank, blank[:24]], axis=0))[:32]
    old_norm, curvature, mixed, image_norm = (packed[:, n:n + 1] for n in range(4))
    step = old_norm / curvature
    new_norm = old_norm - 2.0 * step * mixed + step * step * image_norm
    lane = lax.broadcasted_iota(jnp.int32, (32, 128), 1)
    image_ref[...] = image
    factors_ref[...] = jnp.where(lane == 0, step, new_norm / old_norm)

    all_of(grow, 0, HALF - 1, gc_send)
    all_of(grow, 0, HALF, gr_send)
    all_of(grow, 0, HALF, fw_send)
    all_of(co, 0, LATE - 1, rc_send)
    all_of(ro, 0, HALF - 3, rr_send)
    all_of(late, 0, 6, late_send)
    all_of(st1, 0, GROUP - 1, s1_send)
    all_of(st2, 0, GROUP - 1, s2_send)


def per_device(points, lengthscale, weekday, solution, residual, direction):
    count, feats = points.shape
    probes = direction.shape[1]
    out = jax.ShapeDtypeStruct((probes, count), f32)
    dma = pltpu.SemaphoreType.DMA
    vmem = pltpu.VMEM
    image, factors = pl.pallas_call(
        step_kernel,
        out_shape=[out, jax.ShapeDtypeStruct((probes, 128), f32)],
        in_specs=[pl.BlockSpec(memory_space=pl.ANY)] * 5,
        out_specs=[pl.BlockSpec(memory_space=vmem)] * 2,
        scratch_shapes=[
            vmem((feats, count), f32), vmem((1, feats), f32), vmem((1, count), jnp.int32),
            vmem((probes, count), f32), vmem((probes, count), f32),
            dma((5,)),
            vmem((GROUP, PACK, count), bf16),
            vmem((HALF + 1, SENT, count), bf16),
            vmem((AWAY + 1, count, 128), bf16),
            vmem((HALF + 1, count, 128), bf16),
            vmem((count // 2, count), f32),
            vmem((count // 2, count), f32),
            vmem((count // 2, count), bf16),
            vmem((count // 2, count), bf16),
            vmem((HALF + 1, probes, count), f32),
            vmem((GROUP, probes, count), f32),
            vmem((HALF + 1, probes, count), f32),
            vmem((GROUP, probes, count), f32),
            vmem((6, probes, count), bf16),
            vmem((6, probes, count), bf16),
            vmem((2, 8, 128), f32),
            vmem((GROUP, 8, 128), f32),
            vmem((GROUP, 8, 128), f32),
            dma, dma((GROUP,)), dma, dma, dma((HALF + 1,)),
            dma, dma, dma, dma, dma, dma, dma, dma, dma, dma,
        ],
        compiler_params=pltpu.CompilerParams(
            collective_id=0, has_side_effects=True, vmem_limit_bytes=48 * 2**20),
        name="cg_step",
    )(points.T, lengthscale[None, :], weekday[None, :], residual.T, direction.T)
    step, ratio = factors[:, 0:1], factors[:, 1:2]
    new_residual = residual.T - step * image
    new_solution = solution.T + step * direction.T
    new_direction = new_residual + ratio * direction.T
    return new_solution.T, new_residual.T, new_direction.T


def solution(mesh):
    split = P(("row", "col"), None)
    in_specs = (split, P(), P(("row", "col")), split, split, split)
    return jax.shard_map(
        per_device, mesh=mesh, in_specs=in_specs, out_specs=(split, split, split), check_vma=False
    )
```

```python
import functools

import jax
import jax.numpy as jnp
from jax import lax
from jax.experimental import pallas as pl
from jax.experimental.pallas import tpu as pltpu
from jax.sharding import PartitionSpec as P

f32 = jnp.float32
bf16 = jnp.bfloat16
MESH = pl.DeviceIdType.MESH

root_five = 2.23606797749979
log2_e = 1.4426950408889634
noise_level = 0.5
cross_day = 0.4

FEATS = 32
MISC = 64
SENT = 80
PACK = 112
DEPTH = PACK - FEATS
GROUP = 16
HALF = 8
STRETCH = 5.0 / 3.0 * log2_e
X_PER_ROOT = -(3.0 * log2_e) ** 0.5
OUT_SCALE = cross_day / log2_e
SAME_DAY = 1.0 / cross_day
AWAY = HALF + 1
FAR = 1e6
LONG = 81
TILES = 129
LATE = 13
TINY = 1e-30


def kernel_values(m, row_days, col_days):
    x = (m * X_PER_ROOT) * lax.rsqrt(m)
    p = m - (x - log2_e)
    k = (jnp.exp2(x) * p).astype(bf16)
    return k * jnp.where(row_days == col_days, bf16(SAME_DAY), bf16(1.0))


def step_kernel(
    pts_any, ls_any, day_any, res_any, dir_any,
    image_ref, factors_ref,
    pts_ref, ls_ref, day_ref, res_ref, dir_ref, load,
    gcol, grow, xa, da, v0, v1, k0, k1, ro, co, rrow, rcol, late, landed, stat, st1, st2,
    gc_send, gc_recv, fw_send, gr_send, gr_recv, rr_send, rr_recv, rc_send, rc_recv,
    s1_send, s1_recv, s2_send, s2_recv, late_send, late_recv,
):
    r = lax.axis_index("row")
    c = lax.axis_index("col")

    def at_row(d):
        return (lax.rem(r + d, GROUP), c)

    def at_col(d):
        return (r, lax.rem(c + d + GROUP, GROUP))

    loads = [
        pltpu.make_async_copy(src, dst, load.at[n])
        for n, (src, dst) in enumerate((
            (ls_any, ls_ref), (pts_any, pts_ref), (day_any, day_ref),
            (dir_any, dir_ref), (res_any, res_ref)))
    ]
    for copy in loads:
        copy.start()

    barrier = pltpu.get_barrier_semaphore()

    def greet(d, _):
        pl.semaphore_signal(barrier, inc=1, device_id=at_row(d), device_id_type=MESH)
        pl.semaphore_signal(barrier, inc=1, device_id=at_col(d), device_id_type=MESH)
        return 0

    lax.fori_loop(1, GROUP, greet, 0)

    sent = pl.ds(0, SENT)

    def gather_col(d):
        return pltpu.make_async_remote_copy(
            src_ref=gcol.at[0, sent], dst_ref=gcol.at[d, sent], send_sem=gc_send,
            recv_sem=gc_recv.at[d], device_id=at_row(GROUP - d), device_id_type=MESH)

    side = 1 - 2 * lax.rem(r, 2)

    def forward(d):
        slot = lax.rem(d - side + GROUP, GROUP)
        return pltpu.make_async_remote_copy(
            src_ref=gcol.at[d, sent], dst_ref=gcol.at[slot, sent], send_sem=fw_send,
            recv_sem=gc_recv.at[slot], device_id=at_row(side + GROUP), device_id_type=MESH)

    def turn(d):
        return d * (2 * lax.rem(d, 2) - 1)

    def gather_row(d):
        return pltpu.make_async_remote_copy(
            src_ref=gcol.at[0, sent], dst_ref=grow.at[d], send_sem=gr_send,
            recv_sem=gr_recv.at[d], device_id=at_col(-turn(d)), device_id_type=MESH)

    def give_row(d):
        return pltpu.make_async_remote_copy(
            src_ref=ro.at[d], dst_ref=rrow.at[d], send_sem=rr_send,
            recv_sem=rr_recv, device_id=at_col(turn(d)), device_id_type=MESH)

    def give_col(d):
        return pltpu.make_async_remote_copy(
            src_ref=co.at[d], dst_ref=rcol.at[d], send_sem=rc_send,
            recv_sem=rc_recv, device_id=at_row(d), device_id_type=MESH)

    def give_late(n, ref, d, place):
        late[n] = ref[d].astype(bf16)
        pltpu.make_async_remote_copy(
            src_ref=late.at[n], dst_ref=landed.at[n], send_sem=late_send,
            recv_sem=late_recv, device_id=place, device_id_type=MESH).start()

    def late_row(d):
        give_late(d - 1, ro, d, at_col(turn(d)))

    def late_col(d):
        give_late(d - LATE + 3, co, d, at_row(d))

    def share_row(d):
        return pltpu.make_async_remote_copy(
            src_ref=stat.at[0], dst_ref=st1.at[d], send_sem=s1_send,
            recv_sem=s1_recv, device_id=at_row(d), device_id_type=MESH)

    def share_col(d):
        return pltpu.make_async_remote_copy(
            src_ref=stat.at[1], dst_ref=st2.at[d], send_sem=s2_send,
            recv_sem=s2_recv, device_id=at_col(d), device_id_type=MESH)

    for copy in loads[:4]:
        copy.wait()
    direction = dir_ref[...]
    scales = jnp.transpose(jnp.broadcast_to(ls_ref[...], (128, 32)))[:, :1]
    scaled = (pts_ref[...] / scales).astype(bf16)
    wide = scaled.astype(f32)
    norm = jnp.sum(wide * wide, axis=0, keepdims=True) * STRETCH
    norm_hi = norm.astype(bf16).astype(f32)
    rest = norm - norm_hi
    norm_mid = rest.astype(bf16).astype(f32)
    norm_lo = rest - norm_mid
    points = norm.shape[1]
    line = lax.broadcasted_iota(jnp.int32, (16, points), 0)
    misc = jnp.where(line == 0, norm_hi, 0.0)
    misc = jnp.where(line == 1, norm_mid, misc)
    misc = jnp.where(line == 2, norm_lo, misc)
    misc = jnp.where((line >= 3) & (line < 6), 1.0, misc)
    misc = jnp.where(line == 6, day_ref[...].astype(f32), misc)
    for own in (gcol, grow):
        own[0, :FEATS, :] = direction.astype(bf16)
        own[0, FEATS:MISC, :] = scaled
        own[0, MISC:SENT, :] = misc.astype(bf16)
    gcol[0, SENT:, :] = scaled

    ro[...] = jnp.zeros_like(ro)
    co[...] = jnp.zeros_like(co)

    def prepare(i):
        extra = grow[i, MISC:SENT, :].astype(f32)
        ones = jnp.where(line < 3, 1.0, jnp.where(line < 6, pltpu.roll(extra, 3, 0), 0.0))
        left = grow[i, FEATS:MISC, :].astype(f32) * (-2.0 * STRETCH)
        high = left.astype(bf16).astype(f32)
        block = jnp.concatenate(
            [high, ones, left - high, jnp.zeros((128 - DEPTH, points), f32)], axis=0)
        xa[i] = jnp.transpose(block).astype(bf16)
        da[i] = jnp.transpose(jnp.broadcast_to(extra[6:7, :], (128, points))).astype(bf16)

    rows = points // 2
    halves = (slice(0, rows), slice(rows, points))

    def distances(v, i, j, h):
        squared = jnp.dot(xa[i, halves[h], :DEPTH], gcol[j, FEATS:, :], preferred_element_type=f32)
        v[...] = jnp.maximum(squared, TINY)

    def values(v, k, i, j, h):
        days = jnp.concatenate([da[i, halves[h], :]] * (points // 128), axis=1)
        k[...] = kernel_values(v[...], days, gcol[j, MISC + 6:MISC + 7, :])

    def apply(k, i, j, h):
        row_part = lax.dot_general(
            gcol[j, :FEATS, :], k[...], (((1,), (1,)), ((), ())), preferred_element_type=f32)
        col_part = jnp.dot(grow[i, :FEATS, halves[h]], k[...], preferred_element_type=f32)
        ro[i, :, halves[h]] += row_part
        co[j] += col_part

    def early_place(t):
        p = lax.rem(t + HALF, GROUP)
        q = lax.rem(p, HALF)
        line = lax.div(t + HALF, GROUP)
        shift = jnp.where(t < HALF, 4, 0)
        return (
            jnp.where(t < HALF, 0, 3 + line),
            p - q + lax.rem(2 * q + shift, HALF) + lax.div(q, 4))

    def late_place(t):
        turned = lax.rem(t - LONG, 12)
        return (
            1 + lax.div(turned, 4),
            lax.rem(4 * lax.div(t - LONG, 12) + lax.rem(turned, 4) + 1, GROUP))

    prepare(0)
    for h in range(2):
        distances(v0, 0, 0, h)
        values(v0, k0, 0, 0, h)
        co[0] += jnp.dot(grow[0, :FEATS, halves[h]], k0[...], preferred_element_type=f32)
    k1[...] = jnp.zeros_like(k1)
    lane = lax.broadcasted_iota(jnp.int32, (points, 128), 1)
    xa[AWAY] = jnp.where(lane == MISC - FEATS + 3, FAR, 0.0).astype(bf16)

    pl.semaphore_wait(barrier, 2 * (GROUP - 1))

    def send_col(n, _):
        gather_col(2 * n).start()
        return 0

    forward(0).start()
    for n in (6, 7, 4, 5):
        send_col(n, 0)
    gather_row(4).start()
    lax.fori_loop(1, HALF // 2, send_col, 0)

    def left_of(t, i):
        along_row = (t == 2) | (t == LONG - 1)
        gone = (along_row & (r >= HALF)) | ((t == LONG - 9) & (c >= HALF))
        return jnp.where(gone, AWAY, i)

    def arrived(j):
        gather_col(j).wait_recv()
        gcol[j, SENT:, :] = gcol[j, FEATS:MISC, :]

        @pl.when(lax.rem(j, 2) == 0)
        def _():
            forward(j).start()

    arrived(HALF + 4)
    distances(v0, 0, HALF + 4, 0)

    def early(m, places):
        t = 2 * m
        tile1 = i1, j1 = early_place(t + 1)
        i2, j2 = early_place(t + 2)

        @pl.when(t < GROUP)
        def _():
            arrived(j1)

            @pl.when((t != HALF - 2) & (t != GROUP - 2))
            def _():
                arrived(j2)

        @pl.when(lax.rem(t, GROUP) == HALF - 2)
        def _():
            gather_row(i2).wait_recv()

            @pl.when(i2 < HALF)
            def _():
                gather_row(i2 + 1).start()

            @pl.when(i2 == HALF - 1)
            def _():
                for n in (1, 2, 3):
                    gather_row(n).start()

            @pl.when(i2 > 5)
            def _():
                give_row(i2 - 2).start()

            prepare(i2)

        left2 = left_of(t + 2, i2)
        two_tiles(places, tile1, (left2, i2, j2))
        return i1, j1, left2, i2, j2

    def two_tiles(places, tile1, tile2):
        i_, j_, left0, i0, j0 = places
        i1, j1 = tile1
        left2, i2, j2 = tile2

        apply(k1, i_, j_, 1)
        distances(v1, left0, j0, 1)
        values(v0, k0, i0, j0, 0)
        apply(k0, i0, j0, 0)
        distances(v0, i1, j1, 0)
        values(v1, k1, i0, j0, 1)
        apply(k1, i0, j0, 1)
        distances(v1, i1, j1, 1)
        values(v0, k0, i1, j1, 0)
        apply(k0, i1, j1, 0)
        distances(v0, left2, j2, 0)
        values(v1, k1, i1, j1, 1)

    def late_tiles(m, places):
        t = 2 * m
        i_, j_, _, i0, j0 = places
        tile1 = i1, j1 = late_place(t + 1)
        i2, j2 = late_place(t + 2)
        two_tiles(places, tile1, (i2, i2, j2))

        for i, j in ((i_, j_), (i0, j0)):
            @pl.when((i == 3) & (j < LATE))
            def _(j=j):
                give_col(j).start()

        for done, send in (
            (LONG - 1, lambda: give_row(8).start()),
            (TILES - 9, lambda: late_row(1)),
            (TILES - 5, lambda: late_row(2)),
            (TILES - 3, lambda: (late_col(LATE), late_col(LATE + 1))),
        ):
            pl.when(t == done)(lambda send=send: (send(), None)[1])

        return i1, j1, i2, i2, j2

    begin = jnp.int32(0)
    places = (begin, begin, begin, begin, begin + HALF + 4)
    places = lax.fori_loop(0, LONG // 2, early, places)
    for n in (1, 2, 3):
        gather_row(n).wait_recv()
        prepare(n)
    give_row(7).start()
    lax.fori_loop(LONG // 2, TILES // 2, late_tiles, places)
    apply(k1, 3, GROUP - 1, 1)
    distances(v1, 3, 0, 1)
    values(v0, k0, 3, 0, 0)
    late_col(GROUP - 1)
    apply(k0, 3, 0, 0)
    values(v1, k1, 3, 0, 1)
    apply(k1, 3, 0, 1)
    late_row(3)

    def all_of(ref, start, count, sem):
        part = ref.at[pl.ds(start, count)]
        pltpu.make_async_copy(part, part, sem).wait()

    all_of(rcol, 1, LATE - 1, rc_recv)
    all_of(rrow, 4, HALF - 3, rr_recv)
    applied = ro[0] + co[0]
    for n in range(1, LATE):
        applied = applied + rcol[n]
    for n in range(4, HALF + 1):
        applied = applied + rrow[n]
    all_of(landed, 0, 6, late_recv)
    for n in range(6):
        applied = applied + landed[n].astype(f32)

    image = applied * OUT_SCALE + noise_level * direction
    for copy in loads[4:]:
        copy.wait()
    residual = res_ref[...]
    lane = lax.broadcasted_iota(jnp.int32, (32, 128), 1)
    blank = jnp.zeros((96, 128), f32)
    sums = [residual * residual, direction * image, residual * image, image * image]
    sums = [jnp.sum(v, axis=1, keepdims=True) for v in sums]
    packed = jnp.where(lane == 0, sums[0], jnp.where(lane == 1, sums[1], jnp.where(lane == 2, sums[2], sums[3])))

    def exchange(slot, packed, copy, landing, sem):
        stat[slot] = packed

        def begin(d, _):
            copy(d).start()
            return 0

        lax.fori_loop(1, GROUP, begin, 0)
        all_of(landing, 1, GROUP - 1, sem)
        for n in range(1, GROUP):
            packed = packed + landing[n]
        return packed

    packed = jnp.transpose(jnp.concatenate([packed, blank], axis=0))[:8]
    packed = exchange(0, packed, share_row, st1, s1_recv)
    packed = exchange(1, packed, share_col, st2, s2_recv)
    packed = jnp.transpose(jnp.concatenate([packed, blank, blank[:24]], axis=0))[:32]
    old_norm, curvature, mixed, image_norm = (packed[:, n:n + 1] for n in range(4))
    step = old_norm / curvature
    new_norm = old_norm - 2.0 * step * mixed + step * step * image_norm
    lane = lax.broadcasted_iota(jnp.int32, (32, 128), 1)
    image_ref[...] = image
    factors_ref[...] = jnp.where(lane == 0, step, new_norm / old_norm)

    all_of(grow, 0, HALF - 1, gc_send)
    all_of(grow, 0, HALF, gr_send)
    all_of(grow, 0, HALF, fw_send)
    all_of(co, 0, LATE - 1, rc_send)
    all_of(ro, 0, HALF - 3, rr_send)
    all_of(late, 0, 6, late_send)
    all_of(st1, 0, GROUP - 1, s1_send)
    all_of(st2, 0, GROUP - 1, s2_send)


def per_device(points, lengthscale, weekday, solution, residual, direction):
    count, feats = points.shape
    probes = direction.shape[1]
    out = jax.ShapeDtypeStruct((probes, count), f32)
    dma = pltpu.SemaphoreType.DMA
    vmem = pltpu.VMEM
    image, factors = pl.pallas_call(
        step_kernel,
        out_shape=[out, jax.ShapeDtypeStruct((probes, 128), f32)],
        in_specs=[pl.BlockSpec(memory_space=pl.ANY)] * 5,
        out_specs=[pl.BlockSpec(memory_space=vmem)] * 2,
        scratch_shapes=[
            vmem((feats, count), f32), vmem((1, feats), f32), vmem((1, count), jnp.int32),
            vmem((probes, count), f32), vmem((probes, count), f32),
            dma((5,)),
            vmem((GROUP, PACK, count), bf16),
            vmem((HALF + 1, SENT, count), bf16),
            vmem((AWAY + 1, count, 128), bf16),
            vmem((HALF + 1, count, 128), bf16),
            vmem((count // 2, count), f32),
            vmem((count // 2, count), f32),
            vmem((count // 2, count), bf16),
            vmem((count // 2, count), bf16),
            vmem((HALF + 1, probes, count), f32),
            vmem((GROUP, probes, count), f32),
            vmem((HALF + 1, probes, count), f32),
            vmem((GROUP, probes, count), f32),
            vmem((6, probes, count), bf16),
            vmem((6, probes, count), bf16),
            vmem((2, 8, 128), f32),
            vmem((GROUP, 8, 128), f32),
            vmem((GROUP, 8, 128), f32),
            dma, dma((GROUP,)), dma, dma, dma((HALF + 1,)),
            dma, dma, dma, dma, dma, dma, dma, dma, dma, dma,
        ],
        compiler_params=pltpu.CompilerParams(
            collective_id=0, has_side_effects=True, vmem_limit_bytes=62 * 2**20),
        name="cg_step",
    )(points.T, lengthscale[None, :], weekday[None, :], residual.T, direction.T)
    step, ratio = factors[:, 0:1], factors[:, 1:2]
    new_residual = residual.T - step * image
    new_solution = solution.T + step * direction.T
    new_direction = new_residual + ratio * direction.T
    return new_solution.T, new_residual.T, new_direction.T


def solution(mesh):
    split = P(("row", "col"), None)
    in_specs = (split, P(), P(("row", "col")), split, split, split)
    return jax.shard_map(
        per_device, mesh=mesh, in_specs=in_specs, out_specs=(split, split, split), check_vma=False
    )
```

```python
import functools

import jax
import jax.numpy as jnp
from jax import lax
from jax.experimental import pallas as pl
from jax.experimental.pallas import tpu as pltpu
from jax.sharding import PartitionSpec as P

f32 = jnp.float32
bf16 = jnp.bfloat16
MESH = pl.DeviceIdType.MESH

root_five = 2.23606797749979
log2_e = 1.4426950408889634
noise_level = 0.5
cross_day = 0.4

FEATS = 32
MISC = 64
SENT = 80
PACK = 112
DEPTH = PACK - FEATS
GROUP = 16
HALF = 8
STRETCH = 5.0 / 3.0 * log2_e
X_PER_ROOT = -(3.0 * log2_e) ** 0.5
OUT_SCALE = cross_day / log2_e
SAME_DAY = 1.0 / cross_day
AWAY = HALF + 1
FAR = 1e6
LONG = 81
TILES = 129
LATE = 13
TINY = 1e-30


def kernel_values(m, row_days, col_days):
    x = (m * X_PER_ROOT) * lax.rsqrt(m)
    p = m - (x - log2_e)
    k = (jnp.exp2(x) * p).astype(bf16)
    return k * jnp.where(row_days == col_days, bf16(SAME_DAY), bf16(1.0))


def step_kernel(
    pts_any, ls_any, day_any, res_any, dir_any,
    image_ref, factors_ref,
    pts_ref, ls_ref, day_ref, res_ref, dir_ref, load,
    gcol, grow, xa, da, v0, v1, k0, k1, ro, co, rrow, rcol, late, landed, stat, st1, st2,
    gc_send, gc_recv, fw_send, gr_send, gr_recv, rr_send, rr_recv, rc_send, rc_recv,
    s1_send, s1_recv, s2_send, s2_recv, late_send, late_recv,
):
    r = lax.axis_index("row")
    c = lax.axis_index("col")

    def at_row(d):
        return (lax.rem(r + d, GROUP), c)

    def at_col(d):
        return (r, lax.rem(c + d + GROUP, GROUP))

    loads = [
        pltpu.make_async_copy(src, dst, load.at[n])
        for n, (src, dst) in enumerate((
            (ls_any, ls_ref), (pts_any, pts_ref), (day_any, day_ref),
            (dir_any, dir_ref), (res_any, res_ref)))
    ]
    for copy in loads:
        copy.start()

    barrier = pltpu.get_barrier_semaphore()

    def greet(d, _):
        pl.semaphore_signal(barrier, inc=1, device_id=at_row(d), device_id_type=MESH)
        pl.semaphore_signal(barrier, inc=1, device_id=at_col(d), device_id_type=MESH)
        return 0

    lax.fori_loop(1, GROUP, greet, 0)

    sent = pl.ds(0, SENT)

    def gather_col(d):
        return pltpu.make_async_remote_copy(
            src_ref=gcol.at[0, sent], dst_ref=gcol.at[d, sent], send_sem=gc_send,
            recv_sem=gc_recv.at[d], device_id=at_row(GROUP - d), device_id_type=MESH)

    side = 1 - 2 * lax.rem(r, 2)

    def forward(d):
        slot = lax.rem(d - side + GROUP, GROUP)
        return pltpu.make_async_remote_copy(
            src_ref=gcol.at[d, sent], dst_ref=gcol.at[slot, sent], send_sem=fw_send,
            recv_sem=gc_recv.at[slot], device_id=at_row(side + GROUP), device_id_type=MESH)

    def turn(d):
        return d * (2 * lax.rem(d, 2) - 1)

    def gather_row(d):
        return pltpu.make_async_remote_copy(
            src_ref=gcol.at[0, sent], dst_ref=grow.at[d], send_sem=gr_send,
            recv_sem=gr_recv.at[d], device_id=at_col(-turn(d)), device_id_type=MESH)

    def give_row(d):
        return pltpu.make_async_remote_copy(
            src_ref=ro.at[d], dst_ref=rrow.at[d], send_sem=rr_send,
            recv_sem=rr_recv, device_id=at_col(turn(d)), device_id_type=MESH)

    def give_col(d):
        return pltpu.make_async_remote_copy(
            src_ref=co.at[d], dst_ref=rcol.at[d], send_sem=rc_send,
            recv_sem=rc_recv, device_id=at_row(d), device_id_type=MESH)

    def give_late(n, ref, d, place):
        late[n] = ref[d].astype(bf16)
        pltpu.make_async_remote_copy(
            src_ref=late.at[n], dst_ref=landed.at[n], send_sem=late_send,
            recv_sem=late_recv, device_id=place, device_id_type=MESH).start()

    def late_row(d):
        give_late(d - 1, ro, d, at_col(turn(d)))

    def late_col(d):
        give_late(d - LATE + 3, co, d, at_row(d))

    def share_row(d):
        return pltpu.make_async_remote_copy(
            src_ref=stat.at[0], dst_ref=st1.at[d], send_sem=s1_send,
            recv_sem=s1_recv, device_id=at_row(d), device_id_type=MESH)

    def share_col(d):
        return pltpu.make_async_remote_copy(
            src_ref=stat.at[1], dst_ref=st2.at[d], send_sem=s2_send,
            recv_sem=s2_recv, device_id=at_col(d), device_id_type=MESH)

    for copy in loads[:4]:
        copy.wait()
    direction = dir_ref[...]
    scales = jnp.transpose(jnp.broadcast_to(ls_ref[...], (128, 32)))[:, :1]
    scaled = (pts_ref[...] / scales).astype(bf16)
    wide = scaled.astype(f32)
    norm = jnp.sum(wide * wide, axis=0, keepdims=True) * STRETCH
    norm_hi = norm.astype(bf16).astype(f32)
    rest = norm - norm_hi
    norm_mid = rest.astype(bf16).astype(f32)
    norm_lo = rest - norm_mid
    points = norm.shape[1]
    line = lax.broadcasted_iota(jnp.int32, (16, points), 0)
    misc = jnp.where(line == 0, norm_hi, 0.0)
    misc = jnp.where(line == 1, norm_mid, misc)
    misc = jnp.where(line == 2, norm_lo, misc)
    misc = jnp.where((line >= 3) & (line < 6), 1.0, misc)
    misc = jnp.where(line == 6, day_ref[...].astype(f32), misc)
    for own in (gcol, grow):
        own[0, :FEATS, :] = direction.astype(bf16)
        own[0, FEATS:MISC, :] = scaled
        own[0, MISC:SENT, :] = misc.astype(bf16)
    gcol[0, SENT:, :] = scaled

    ro[...] = jnp.zeros_like(ro)
    co[...] = jnp.zeros_like(co)

    def prepare(i):
        extra = grow[i, MISC:SENT, :].astype(f32)
        ones = jnp.where(line < 3, 1.0, jnp.where(line < 6, pltpu.roll(extra, 3, 0), 0.0))
        left = grow[i, FEATS:MISC, :].astype(f32) * (-2.0 * STRETCH)
        high = left.astype(bf16).astype(f32)
        block = jnp.concatenate(
            [high, ones, left - high, jnp.zeros((128 - DEPTH, points), f32)], axis=0)
        xa[i] = jnp.transpose(block).astype(bf16)
        da[i] = jnp.transpose(jnp.broadcast_to(extra[6:7, :], (128, points))).astype(bf16)

    rows = points // 2
    halves = (slice(0, rows), slice(rows, points))

    def distances(v, i, j, h):
        squared = jnp.dot(xa[i, halves[h], :DEPTH], gcol[j, FEATS:, :], preferred_element_type=f32)
        v[...] = jnp.maximum(squared, TINY)

    def values(v, k, i, j, h):
        days = jnp.concatenate([da[i, halves[h], :]] * (points // 128), axis=1)
        k[...] = kernel_values(v[...], days, gcol[j, MISC + 6:MISC + 7, :])

    def apply(k, i, j, h):
        row_part = lax.dot_general(
            gcol[j, :FEATS, :], k[...], (((1,), (1,)), ((), ())), preferred_element_type=f32)
        col_part = jnp.dot(grow[i, :FEATS, halves[h]], k[...], preferred_element_type=f32)
        ro[i, :, halves[h]] += row_part
        co[j] += col_part

    def early_place(t):
        p = lax.rem(t + HALF, GROUP)
        q = lax.rem(p, HALF)
        line = lax.div(t + HALF, GROUP)
        shift = jnp.where(t < HALF, 4, 0)
        return (
            jnp.where(t < HALF, 0, 3 + line),
            p - q + lax.rem(2 * q + shift, HALF) + lax.div(q, 4))

    def late_place(t):
        turned = lax.rem(t - LONG, 12)
        return (
            1 + lax.div(turned, 4),
            lax.rem(4 * lax.div(t - LONG, 12) + lax.rem(turned, 4) + 1, GROUP))

    prepare(0)
    for h in range(2):
        distances(v0, 0, 0, h)
        values(v0, k0, 0, 0, h)
        co[0] += jnp.dot(grow[0, :FEATS, halves[h]], k0[...], preferred_element_type=f32)
    k1[...] = jnp.zeros_like(k1)
    lane = lax.broadcasted_iota(jnp.int32, (points, 128), 1)
    xa[AWAY] = jnp.where(lane == MISC - FEATS + 3, FAR, 0.0).astype(bf16)

    pl.semaphore_wait(barrier, 2 * (GROUP - 1))

    def send_col(n, _):
        gather_col(2 * n).start()
        return 0

    forward(0).start()
    for n in (6, 7, 4, 5):
        send_col(n, 0)
    gather_row(4).start()
    lax.fori_loop(1, HALF // 2, send_col, 0)

    def left_of(t, i):
        along_row = (t == 2) | (t == LONG - 1)
        gone = (along_row & (r >= HALF)) | ((t == LONG - 9) & (c >= HALF))
        return jnp.where(gone, AWAY, i)

    def arrived(j):
        gather_col(j).wait_recv()

        @pl.when(lax.rem(j, 2) == 0)
        def _():
            forward(j).start()

        gcol[j, SENT:, :] = gcol[j, FEATS:MISC, :]

    arrived(HALF + 4)
    distances(v0, 0, HALF + 4, 0)

    def early(m, places):
        t = 2 * m
        tile1 = i1, j1 = early_place(t + 1)
        i2, j2 = early_place(t + 2)

        @pl.when(t < GROUP)
        def _():
            arrived(j1)

            @pl.when((t != HALF - 2) & (t != GROUP - 2))
            def _():
                arrived(j2)

        @pl.when(lax.rem(t, GROUP) == HALF - 2)
        def _():
            gather_row(i2).wait_recv()

            @pl.when(i2 < HALF)
            def _():
                gather_row(i2 + 1).start()

            @pl.when(i2 == HALF - 1)
            def _():
                for n in (1, 2, 3):
                    gather_row(n).start()

            @pl.when(i2 > 5)
            def _():
                give_row(i2 - 2).start()

            prepare(i2)

        left2 = left_of(t + 2, i2)
        two_tiles(places, tile1, (left2, i2, j2))
        return i1, j1, left2, i2, j2

    def two_tiles(places, tile1, tile2):
        i_, j_, left0, i0, j0 = places
        i1, j1 = tile1
        left2, i2, j2 = tile2

        apply(k1, i_, j_, 1)
        distances(v1, left0, j0, 1)
        values(v0, k0, i0, j0, 0)
        apply(k0, i0, j0, 0)
        distances(v0, i1, j1, 0)
        values(v1, k1, i0, j0, 1)
        apply(k1, i0, j0, 1)
        distances(v1, i1, j1, 1)
        values(v0, k0, i1, j1, 0)
        apply(k0, i1, j1, 0)
        distances(v0, left2, j2, 0)
        values(v1, k1, i1, j1, 1)

    def late_tiles(m, places):
        t = 2 * m
        i_, j_, _, i0, j0 = places
        tile1 = i1, j1 = late_place(t + 1)
        i2, j2 = late_place(t + 2)
        two_tiles(places, tile1, (i2, i2, j2))

        for i, j in ((i_, j_), (i0, j0)):
            @pl.when((i == 3) & (j < LATE))
            def _(j=j):
                give_col(j).start()

        for done, send in (
            (LONG - 1, lambda: give_row(8).start()),
            (TILES - 9, lambda: late_row(1)),
            (TILES - 5, lambda: late_row(2)),
            (TILES - 3, lambda: (late_col(LATE), late_col(LATE + 1))),
        ):
            pl.when(t == done)(lambda send=send: (send(), None)[1])

        return i1, j1, i2, i2, j2

    begin = jnp.int32(0)
    places = (begin, begin, begin, begin, begin + HALF + 4)
    places = lax.fori_loop(0, LONG // 2, early, places)
    for n in (1, 2, 3):
        gather_row(n).wait_recv()
        prepare(n)
    give_row(7).start()
    lax.fori_loop(LONG // 2, TILES // 2, late_tiles, places)
    apply(k1, 3, GROUP - 1, 1)
    distances(v1, 3, 0, 1)
    values(v0, k0, 3, 0, 0)
    late_col(GROUP - 1)
    apply(k0, 3, 0, 0)
    values(v1, k1, 3, 0, 1)
    apply(k1, 3, 0, 1)
    late_row(3)

    def all_of(ref, start, count, sem):
        part = ref.at[pl.ds(start, count)]
        pltpu.make_async_copy(part, part, sem).wait()

    all_of(rcol, 1, LATE - 1, rc_recv)
    all_of(rrow, 4, HALF - 3, rr_recv)
    applied = ro[0] + co[0]
    for n in range(1, LATE):
        applied = applied + rcol[n]
    for n in range(4, HALF + 1):
        applied = applied + rrow[n]
    all_of(landed, 0, 6, late_recv)
    for n in range(6):
        applied = applied + landed[n].astype(f32)

    image = applied * OUT_SCALE + noise_level * direction
    for copy in loads[4:]:
        copy.wait()
    residual = res_ref[...]
    lane = lax.broadcasted_iota(jnp.int32, (32, 128), 1)
    blank = jnp.zeros((96, 128), f32)
    sums = [residual * residual, direction * image, residual * image, image * image]
    sums = [jnp.sum(v, axis=1, keepdims=True) for v in sums]
    packed = jnp.where(lane == 0, sums[0], jnp.where(lane == 1, sums[1], jnp.where(lane == 2, sums[2], sums[3])))

    def exchange(slot, packed, copy, landing, sem):
        stat[slot] = packed

        def begin(d, _):
            copy(d).start()
            return 0

        lax.fori_loop(1, GROUP, begin, 0)
        all_of(landing, 1, GROUP - 1, sem)
        for n in range(1, GROUP):
            packed = packed + landing[n]
        return packed

    packed = jnp.transpose(jnp.concatenate([packed, blank], axis=0))[:8]
    packed = exchange(0, packed, share_row, st1, s1_recv)
    packed = exchange(1, packed, share_col, st2, s2_recv)
    packed = jnp.transpose(jnp.concatenate([packed, blank, blank[:24]], axis=0))[:32]
    old_norm, curvature, mixed, image_norm = (packed[:, n:n + 1] for n in range(4))
    step = old_norm / curvature
    new_norm = old_norm - 2.0 * step * mixed + step * step * image_norm
    lane = lax.broadcasted_iota(jnp.int32, (32, 128), 1)
    image_ref[...] = image
    factors_ref[...] = jnp.where(lane == 0, step, new_norm / old_norm)

    all_of(grow, 0, HALF - 1, gc_send)
    all_of(grow, 0, HALF, gr_send)
    all_of(grow, 0, HALF, fw_send)
    all_of(co, 0, LATE - 1, rc_send)
    all_of(ro, 0, HALF - 3, rr_send)
    all_of(late, 0, 6, late_send)
    all_of(st1, 0, GROUP - 1, s1_send)
    all_of(st2, 0, GROUP - 1, s2_send)


def per_device(points, lengthscale, weekday, solution, residual, direction):
    count, feats = points.shape
    probes = direction.shape[1]
    out = jax.ShapeDtypeStruct((probes, count), f32)
    dma = pltpu.SemaphoreType.DMA
    vmem = pltpu.VMEM
    image, factors = pl.pallas_call(
        step_kernel,
        out_shape=[out, jax.ShapeDtypeStruct((probes, 128), f32)],
        in_specs=[pl.BlockSpec(memory_space=pl.ANY)] * 5,
        out_specs=[pl.BlockSpec(memory_space=vmem)] * 2,
        scratch_shapes=[
            vmem((feats, count), f32), vmem((1, feats), f32), vmem((1, count), jnp.int32),
            vmem((probes, count), f32), vmem((probes, count), f32),
            dma((5,)),
            vmem((GROUP, PACK, count), bf16),
            vmem((HALF + 1, SENT, count), bf16),
            vmem((AWAY + 1, count, 128), bf16),
            vmem((HALF + 1, count, 128), bf16),
            vmem((count // 2, count), f32),
            vmem((count // 2, count), f32),
            vmem((count // 2, count), bf16),
            vmem((count // 2, count), bf16),
            vmem((HALF + 1, probes, count), f32),
            vmem((GROUP, probes, count), f32),
            vmem((HALF + 1, probes, count), f32),
            vmem((GROUP, probes, count), f32),
            vmem((6, probes, count), bf16),
            vmem((6, probes, count), bf16),
            vmem((2, 8, 128), f32),
            vmem((GROUP, 8, 128), f32),
            vmem((GROUP, 8, 128), f32),
            dma, dma((GROUP,)), dma, dma, dma((HALF + 1,)),
            dma, dma, dma, dma, dma, dma, dma, dma, dma, dma,
        ],
        compiler_params=pltpu.CompilerParams(
            collective_id=0, has_side_effects=True, vmem_limit_bytes=62 * 2**20),
        name="cg_step",
    )(points.T, lengthscale[None, :], weekday[None, :], residual.T, direction.T)
    step, ratio = factors[:, 0:1], factors[:, 1:2]
    new_residual = residual.T - step * image
    new_solution = solution.T + step * direction.T
    new_direction = new_residual + ratio * direction.T
    return new_solution.T, new_residual.T, new_direction.T


def solution(mesh):
    split = P(("row", "col"), None)
    in_specs = (split, P(), P(("row", "col")), split, split, split)
    return jax.shard_map(
        per_device, mesh=mesh, in_specs=in_specs, out_specs=(split, split, split), check_vma=False
    )
```
